256 devices in a mesh: node: 4 (over x_hi, core), inner: 16 (over x_lo, z), tensor: 4 (over y).
Axes of the slice: x: 4 (x_hi: 2, x_lo: 2; x = x_hi * 2 + x_lo), y: 4, z: 8, core: 2. Of those that a mesh axis runs over, the one named last changes fastest.
Arguments:
- prev_hidden: bfloat16 [8192, 14336], P(('node', 'inner'), 'tensor'), may hold values from -6 to 6
- prev_cot: bfloat16 [8192, 4096], P(('node', 'inner')), may hold values from -16 to 16
- next_hidden: bfloat16 [8192, 14336], P(('node', 'inner'), 'tensor'), may hold values from -6 to 6
- weight: float32 [4096, 14336], P(('node', 'inner'), 'tensor'), may hold values from -0.3 to 0.3
- moment1: float32 [4096, 14336], P(('node', 'inner'), 'tensor'), may hold values from -0.03314563 to 0.03314563
- moment2: float32 [4096, 14336], P(('node', 'inner'), 'tensor'), may hold values from 1.2207031e-05 to 0.0012207031
Outputs:
- ffn_out: bfloat16 [8192, 4096], P(('node', 'inner'), 'tensor')
- new_weight: float32 [4096, 14336], P(('node', 'inner'), 'tensor')
- new_moment1: float32 [4096, 14336], P(('node', 'inner'), 'tensor')
- new_moment2: float32 [4096, 14336], P(('node', 'inner'), 'tensor')
The draws below stay inside these ranges and needn't reach their ends.
All inputs are finite; a program needn't handle non-finite values.
Results may differ from the reference program's by a relative error of at most 0.013.
Values may be sent and summed in bfloat16 or wider, within the bound.
A program may use at most 256 MiB of HBM per device.

```python
import math
import jax
import jax.numpy as jnp
from jax import lax

D = 4096
FB = 14336
ADAM_STEP = 20
ALL_TOKENS = 8192
N_TENSOR = 4


def spiked(drawn, key, source, target, shards_of, factor):
    def block_of(dim):
        return (jnp.arange(drawn.shape[dim]) // (drawn.shape[dim] // shards_of)).reshape((-1,) + (1,) * (drawn.ndim - 1 - dim))

    near = jax.random.permutation(key, shards_of)[block_of(target)]
    far = (block_of(target) + shards_of // 2) % shards_of
    return jnp.where((block_of(source) == near) | (block_of(source) == far), factor * drawn, drawn)


def levels(rng, shape, cuts, low, high):
    gain, own = 1.0, jax.random.fold_in(rng, 6)
    for dim, blocks in cuts:
        draws = jnp.exp(jax.random.uniform(jax.random.fold_in(own, dim), (blocks,), jnp.float32, low / len(cuts), high / len(cuts)))
        gain = gain * jnp.repeat(draws, shape[dim] // blocks).reshape([-1 if axis == dim else 1 for axis in range(len(shape))])
    return gain


def gaussian(stream_key, dims, spread, reach, pieces=(), held_as=jnp.bfloat16):
    entries = spread * jax.random.normal(stream_key, dims, jnp.float32)
    if pieces:
        entries = entries * levels(stream_key, dims, pieces, -0.22, 0.18)
    return jnp.clip(entries, -reach, reach).astype(held_as)


def heavy_noise(own_key, dims, scale, bound, cuts, heavy, kind=jnp.bfloat16):
    array = scale * jax.random.normal(own_key, dims, jnp.float32)
    if cuts:
        array = array * levels(own_key, dims, cuts, -0.22, 0.18)
    return jnp.clip(spiked(array, jax.random.fold_in(own_key, 3), *heavy), -bound, bound).astype(kind)


def setup_inputs(seed: int = 0) -> dict:
    splits = jax.random.split(jax.random.key(seed), 7)
    return {
        "prev_hidden": gaussian(splits[0], (ALL_TOKENS, FB), 1.0, 6.0, ((0, 64), (1, 4))),
        "prev_cot": heavy_noise(splits[1], (ALL_TOKENS, D), 1.0, 16.0, ((0, 64),), (0, 1, 64, 4.0)),
        "next_hidden": gaussian(splits[2], (ALL_TOKENS, FB), 1.0, 6.0, ((0, 64), (1, 4))),
        "weight": gaussian(splits[3], (D, FB), 0.05, 0.3, ((0, 64), (1, 4)), jnp.float32),
        "moment1": gaussian(splits[4], (D, FB), (0.5 * ALL_TOKENS ** -0.5), 0.03314563, ((0, 64), (1, 4)), jnp.float32),
        "moment2": jnp.clip(jnp.exp(math.log(0.0012207031) - 4.6051702 * jax.random.uniform(splits[5], (D, FB), jnp.float32) ** levels(splits[5], (D, FB), ((0, 64), (1, 4)), -0.2, 0.2)), 1.220703143189894e-05, 0.0012207031),
    }


def reference(prev_hidden, prev_cot, next_hidden, weight, moment1, moment2):
    gradient = jnp.dot(prev_cot.T, prev_hidden, preferred_element_type=jnp.float32) / ALL_TOKENS
    new_moment1 = 0.9 * moment1 + 0.1 * gradient
    new_moment2 = 0.95 * moment2 + 0.05 * gradient * gradient
    first_fix = 1.0 - 0.9 ** ADAM_STEP
    second_fix = 1.0 - 0.95 ** ADAM_STEP
    ratio = new_moment1 / first_fix / (jnp.sqrt(new_moment2 / second_fix) + 1e-08)
    new_weight = weight - 0.05 * (ratio + 0.1 * weight)
    weight_copy = new_weight.astype(jnp.bfloat16)
    group_width = FB // N_TENSOR
    scale = 1.0 / FB ** 0.5
    total = jnp.zeros((ALL_TOKENS, D), jnp.float32)
    for group in range(N_TENSOR):
        lower = group * group_width
        hidden_part = next_hidden[:, lower:lower + group_width]
        weight_part = weight_copy[:, lower:lower + group_width]
        partial_value = jnp.dot(hidden_part, weight_part.T, preferred_element_type=jnp.float32) * scale
        rounded = lax.optimization_barrier(partial_value.astype(jnp.bfloat16))
        total = total + rounded.astype(jnp.float32)
    ffn_out = total.astype(jnp.bfloat16)
    return (ffn_out, new_weight, new_moment1, new_moment2)
```

```python
import functools
import math

import jax
import jax.numpy as jnp
from jax import lax
from jax.experimental import pallas as pl
from jax.experimental.pallas import tpu as pltpu
from jax.sharding import PartitionSpec as P

FB = 14336
ADAM_STEP = 20
MESH = pl.DeviceIdType.MESH
XS = 4
CUT = 512
LAG_X = 1
LAG_Z = 1
NEXT_AT = 4


def kernel(
    zs, cut, lag_x, lag_z, next_at,
    hid_ref, cot_ref, nxt_ref, w_ref, m1_ref, m2_ref,
    ffn_ref, nw_ref, nm1_ref, nm2_ref,
    hbuf, xbuf, cbuf, ct, grad, send_p, send_m, recv_p, recv_m, wv, m1v, m2v, wall, acc, part, got, fin,
    x_send, x_recv, x_own, c_send, c_recv, c_own, rs_send, rs_recv, ag_send, ag_recv,
    o_send, o_recv, loads, stores, last,
):
    tok, cols = hid_ref.shape
    rows = w_ref.shape[0]
    n = cols // cut
    steps = zs // 2
    feats = rows * zs
    all_tokens = tok * zs * XS * 2 * 1
    factor = 1.0 / math.sqrt(FB)

    node, inner, ten = lax.axis_index("node"), lax.axis_index("inner"), lax.axis_index("tensor")
    core, x_lo, z = lax.rem(node, 2), lax.div(inner, zs), lax.rem(inner, zs)
    x = lax.div(node, 2) * 2 + x_lo

    def at(px, pz, pc, py):
        return (lax.div(px, 2) * 2 + pc, lax.rem(px, 2) * zs + pz, py)

    def row_peer(j, dc):
        return lax.rem(x + j, XS), lax.rem(core + dc, 2)

    def row_device(j, dc):
        px, pc = row_peer(j, dc)
        return at(px, z, pc, ten)

    def z_device(d):
        return at(x, lax.rem(z + d + zs, zs), core, ten)

    barrier = pltpu.get_barrier_semaphore()
    at_home = node == ten
    for j in range(XS):
        for dc in range(2):
            if j or dc:
                pl.semaphore_signal(barrier, inc=1, device_id=row_device(j, dc), device_id_type=MESH)
    for d in (1, -1):
        pl.semaphore_signal(barrier, inc=1, device_id=z_device(d), device_id_type=MESH)
    for lo in range(2):
        for py in range(4):
            mine = at_home & (x_lo == lo) & (ten == py)

            @pl.when(jnp.logical_not(mine))
            def _():
                pl.semaphore_signal(
                    barrier, inc=1, device_id=(ten, lo * zs + z, jnp.int32(py)), device_id_type=MESH
                )

    load_w = pltpu.make_async_copy(w_ref, wv, loads.at[0])
    load_m1 = pltpu.make_async_copy(m1_ref, m1v, loads.at[1])
    load_m2 = pltpu.make_async_copy(m2_ref, m2v, loads.at[2])

    def block_of(px, pc):
        return (lax.div(px, 2) * 2 + pc) * 2 + lax.rem(px, 2)

    def cot_columns(px, pc):
        return cot_ref.at[:, pl.ds(pl.multiple_of(block_of(px, pc) * feats, feats), feats)]

    own_c = pltpu.make_async_copy(cot_columns(x, core), cbuf.at[0], c_own)

    def c_copy(j, dc):
        px, pc = row_peer(j, dc)
        slot = ((XS - j) % XS) * 2 + dc
        return pltpu.make_async_remote_copy(
            src_ref=cot_columns(px, pc), dst_ref=cbuf.at[slot], send_sem=c_send.at[slot],
            recv_sem=c_recv.at[slot], device_id=at(px, z, pc, ten), device_id_type=MESH,
        )

    def chunk(k):
        return pl.ds(pl.multiple_of(k * cut, cut), cut)

    def x_own_copy(a, k):
        ref, buf = (hid_ref, hbuf) if a == 0 else (nxt_ref, xbuf)
        return pltpu.make_async_copy(ref.at[:, chunk(k)], buf.at[k, 0], x_own.at[a, k])

    def x_copy(a, k, i):
        ref, buf = (hid_ref, hbuf) if a == 0 else (nxt_ref, xbuf)
        half = tok // 2
        first, second = pl.ds(0, half), pl.ds(half, half)
        src, dst, peer = {
            0: (ref.at[:, chunk(k)], buf.at[k, 1], (0, 1)),
            1: (ref.at[:, chunk(k)], buf.at[k, 2], (XS - 1, 0)),
            2: (ref.at[:, chunk(k)], buf.at[k, 6], (1, 0)),
            3: (buf.at[k, 6, first], buf.at[k, 4, first], (1, 0)),
            4: (buf.at[k, 2, second], buf.at[k, 4, second], (XS - 1, 0)),
            5: (buf.at[k, 2], buf.at[k, 3], (0, 1)),
            6: (buf.at[k, 6], buf.at[k, 7], (0, 1)),
            7: (buf.at[k, 4], buf.at[k, 5], (0, 1)),
        }[i]
        return pltpu.make_async_remote_copy(
            src_ref=src, dst_ref=dst, send_sem=x_send.at[a, k, i], recv_sem=x_recv.at[a, k, i],
            device_id=row_device(*peer), device_id_type=MESH,
        )

    half_rows = rows // 2
    part_of = (pl.ds(0, half_rows), pl.ds(half_rows, half_rows))

    def rs_copy(k, d, s):
        src, dst = (send_p, recv_p) if d == 0 else (send_m, recv_m)
        src, dst = src.at[k, s], dst.at[k, s]
        if s == 0:
            src, dst = src.at[part_of[d]], dst.at[part_of[d]]
        return pltpu.make_async_remote_copy(
            src_ref=src, dst_ref=dst, send_sem=rs_send.at[k, d, s], recv_sem=rs_recv.at[k, d, s],
            device_id=z_device(1 - 2 * d), device_id_type=MESH,
        )

    def ag_copy(k, d, s, arriving=False):
        far = s + 1 if arriving else s
        slot = lax.rem(z + (zs - far if d == 0 else far), zs)
        ref = wall.at[k, slot]
        if s == steps - 1:
            ref = ref.at[part_of[d]]
        return pltpu.make_async_remote_copy(
            src_ref=ref, dst_ref=ref, send_sem=ag_send.at[k, d, s], recv_sem=ag_recv.at[k, d, s],
            device_id=z_device(1 - 2 * d), device_id_type=MESH,
        )

    def store(k, i):
        src, dst = ((wv, nw_ref), (m1v, nm1_ref), (m2v, nm2_ref))[i]
        return pltpu.make_async_copy(src.at[:, chunk(k)], dst.at[:, chunk(k)], stores.at[i, k])

    own_c.start()
    load_w.start()
    load_m1.start()
    load_m2.start()
    pl.semaphore_wait(barrier, 7 + 2 + 8 - jnp.where(at_home, 1, 0))
    for j in (2, 1, 3, 0):
        for dc in (0, 1):
            if j or dc:
                c_copy(j, dc).start()
    acc[...] = jnp.zeros_like(acc)

    def x_first(a, k):
        x_own_copy(a, k).start()
        for i in (1, 2, 0):
            x_copy(a, k, i).start()

    def x_second(a, k):
        x_copy(a, k, 2).wait_recv()
        x_copy(a, k, 3).start()
        x_copy(a, k, 1).wait_recv()
        x_copy(a, k, 4).start()
        x_copy(a, k, 5).start()
        x_copy(a, k, 6).start()

    def x_third(a, k):
        x_copy(a, k, 3).wait_recv()
        x_copy(a, k, 4).wait_recv()
        x_copy(a, k, 7).start()

    def x_done(a, k):
        x_own_copy(a, k).wait()
        for i in (0, 5, 6, 7):
            x_copy(a, k, i).wait_recv()

    def multiply(k):
        @pl.when(k == 0)
        def _():
            own_c.wait()
            for j in range(XS):
                for dc in range(2):
                    if j or dc:
                        c_copy(j, dc).wait_recv()
            for slot in range(2 * XS):
                ct[:, slot * tok:(slot + 1) * tok] = cbuf[slot].T

        x_done(0, k)
        block = hbuf[k].reshape(2 * XS * tok, cut)
        tile = min(4, zs)
        for i in range(zs // tile):
            sums = jnp.dot(
                ct[i * tile * rows:(i + 1) * tile * rows, :], block, preferred_element_type=jnp.float32
            )
            grad[k, i * tile:(i + 1) * tile] = sums.reshape(tile, rows, cut)
        opposite = grad[k, lax.rem(z + steps, zs)].astype(jnp.bfloat16)
        send_p[k, 0] = opposite
        send_m[k, 0] = opposite
        rs_copy(k, 0, 0).start()
        rs_copy(k, 1, 0).start()

    def rs_step(k, s):
        for d in range(2):
            src, dst = (send_p, recv_p) if d == 0 else (send_m, recv_m)
            rs_copy(k, d, s - 1).wait_recv()
            far = steps - s
            own = grad.at[k, lax.rem(z + (far if d == 0 else zs - far), zs)]
            if s == 1:
                with_it, without = (0, half_rows) if d == 0 else (half_rows, 0)
                a, b = pl.ds(with_it, half_rows), pl.ds(without, half_rows)
                src[k, s, a] = (own[a] + dst[k, 0, a].astype(jnp.float32)).astype(jnp.bfloat16)
                src[k, s, b] = own[b].astype(jnp.bfloat16)
            else:
                src[k, s] = (own[...] + dst[k, s - 1].astype(jnp.float32)).astype(jnp.bfloat16)
            rs_copy(k, d, s).start()

    def adam(k):
        @pl.when(k == 0)
        def _():
            load_w.wait()
            load_m1.wait()
            load_m2.wait()

        rs_copy(k, 0, steps - 1).wait_recv()
        rs_copy(k, 1, steps - 1).wait_recv()
        summed = (
            grad[k, z]
            + recv_p[k, steps - 1].astype(jnp.float32)
            + recv_m[k, steps - 1].astype(jnp.float32)
        )
        gradient = summed / all_tokens
        here = chunk(k)
        new_moment1 = 0.9 * m1v[:, here] + 0.1 * gradient
        new_moment2 = 0.95 * m2v[:, here] + 0.05 * gradient * gradient
        first_fix = 1.0 - 0.9**ADAM_STEP
        second_fix = 1.0 - 0.95**ADAM_STEP
        ratio = new_moment1 / first_fix / (jnp.sqrt(new_moment2 / second_fix) + 1e-08)
        weight = wv[:, here]
        new_weight = weight - 0.05 * (ratio + 0.1 * weight)
        wall[k, z] = new_weight.astype(jnp.bfloat16)
        ag_copy(k, 0, 0).start()
        ag_copy(k, 1, 0).start()
        wv[:, here] = new_weight
        m1v[:, here] = new_moment1
        m2v[:, here] = new_moment2
        for i in range(3):
            store(k, i).start()

    def ag_step(k, s):
        for d in range(2):
            ag_copy(k, d, s - 1, arriving=True).wait_recv()
            ag_copy(k, d, s).start()

    def forward(k):
        for d in range(2):
            ag_copy(k, d, steps - 1, arriving=True).wait_recv()
        x_done(1, k)
        copy = wall[k].reshape(feats, cut)
        for i in range(XS):
            block = xbuf[k, 2 * i:2 * i + 2].reshape(2 * tok, cut)
            acc[2 * i * tok:2 * (i + 1) * tok, :] += lax.dot_general(
                block, copy, (((1,), (1,)), ((), ())), preferred_element_type=jnp.float32
            )

    at_mul = 3 * lag_x
    at_adam = at_mul + steps * lag_z
    at_out = max(at_adam + steps * lag_z, next_at + 3 * lag_x)
    plan = []
    for s in range(steps - 1, 0, -1):
        plan.append((at_adam + s * lag_z, functools.partial(ag_step, s=s)))
    for s in range(steps - 1, 0, -1):
        plan.append((at_mul + s * lag_z, functools.partial(rs_step, s=s)))
    plan.append((at_adam, adam))
    for a, base in ((0, 0), (1, next_at)):
        plan.append((base + 2 * lag_x, functools.partial(x_third, a)))
        plan.append((base + lag_x, functools.partial(x_second, a)))
        plan.append((base, functools.partial(x_first, a)))
    plan.append((at_mul, multiply))
    plan.append((at_out, forward))

    def tick(t, carry):
        for start, stage in plan:
            k = t - start

            @pl.when((k >= 0) & (k < n))
            def _(k=k, stage=stage):
                stage(k)

        return carry

    lax.fori_loop(0, at_out + n, tick, 0)

    def o_copy(j, dc):
        px, pc = row_peer(j, dc)
        return pltpu.make_async_remote_copy(
            src_ref=part.at[2 * j + dc], dst_ref=got.at[ten * 2 + x_lo], send_sem=o_send.at[2 * j + dc],
            recv_sem=o_recv.at[ten * 2 + x_lo], device_id=at(px, z, pc, node), device_id_type=MESH,
        )

    stay = pltpu.make_async_copy(part.at[0], got.at[ten * 2 + x_lo], o_recv.at[ten * 2 + x_lo])
    for j in (2, 1, 3, 0):
        for dc in range(2):
            slot = 2 * j + dc
            part[slot] = (acc[slot * tok:(slot + 1) * tok, :] * factor).astype(jnp.bfloat16)
            if slot:
                o_copy(j, dc).start()
            else:

                @pl.when(at_home)
                def _():
                    stay.start()

                @pl.when(jnp.logical_not(at_home))
                def _():
                    o_copy(0, 0).start()

    for j in range(XS):
        for dc in range(2):
            if j or dc:
                c_copy(j, dc).wait_send()

    def drain(k, carry):
        for a in range(2):
            for i in range(8):
                x_copy(a, k, i).wait_send()
        for d in range(2):
            for s in range(steps):
                rs_copy(k, d, s).wait_send()
                ag_copy(k, d, s).wait_send()
        for i in range(3):
            store(k, i).wait()
        return carry

    lax.fori_loop(0, n, drain, 0)

    for lo in range(2):
        total = jnp.zeros((tok, feats), jnp.float32)
        for py in range(4):
            slot = 2 * py + lo
            pltpu.make_async_copy(part.at[0], got.at[slot], o_recv.at[slot]).wait()
            total = total + got[slot].astype(jnp.float32)
        fin[:, lo * feats:(lo + 1) * feats] = total.astype(jnp.bfloat16)
    out = pltpu.make_async_copy(fin, ffn_ref, last)
    out.start()
    for j in range(XS):
        for dc in range(2):
            if j or dc:
                o_copy(j, dc).wait_send()

    @pl.when(jnp.logical_not(at_home))
    def _():
        o_copy(0, 0).wait_send()

    out.wait()


def on_device(prev_hidden, prev_cot, next_hidden, weight, moment1, moment2):
    tok, cols = prev_hidden.shape
    rows, features = weight.shape[0], prev_cot.shape[1]
    zs = lax.axis_size("inner") // 2
    steps = zs // 2
    cut = min(CUT, cols // 2)
    n = cols // cut
    feats = rows * zs
    bf16, f32 = jnp.bfloat16, jnp.float32
    dma = pltpu.SemaphoreType.DMA
    anywhere = pl.BlockSpec(memory_space=pl.ANY)
    return pl.pallas_call(
        functools.partial(kernel, zs, cut, LAG_X, LAG_Z, NEXT_AT),
        out_shape=(
            jax.ShapeDtypeStruct((tok, features // 4), bf16),
            jax.ShapeDtypeStruct(weight.shape, f32),
            jax.ShapeDtypeStruct(weight.shape, f32),
            jax.ShapeDtypeStruct(weight.shape, f32),
        ),
        in_specs=[anywhere] * 6,
        out_specs=(anywhere,) * 4,
        scratch_shapes=[
            pltpu.VMEM((n, 2 * XS, tok, cut), bf16),
            pltpu.VMEM((n, 2 * XS, tok, cut), bf16),
            pltpu.VMEM((2 * XS, tok, feats), bf16),
            pltpu.VMEM((feats, 2 * XS * tok), bf16),
            pltpu.VMEM((n, zs, rows, cut), f32),
            pltpu.VMEM((n, steps, rows, cut), bf16),
            pltpu.VMEM((n, steps, rows, cut), bf16),
            pltpu.VMEM((n, steps, rows, cut), bf16),
            pltpu.VMEM((n, steps, rows, cut), bf16),
            pltpu.VMEM((rows, cols), f32),
            pltpu.VMEM((rows, cols), f32),
            pltpu.VMEM((rows, cols), f32),
            pltpu.VMEM((n, zs, rows, cut), bf16),
            pltpu.VMEM((2 * XS * tok, feats), f32),
            pltpu.VMEM((2 * XS, tok, feats), bf16),
            pltpu.VMEM((2 * XS, tok, feats), bf16),
            pltpu.VMEM((tok, 2 * feats), bf16),
            dma((2, n, 8)),
            dma((2, n, 8)),
            dma((2, n)),
            dma((2 * XS,)),
            dma((2 * XS,)),
            dma(()),
            dma((n, 2, steps)),
            dma((n, 2, steps)),
            dma((n, 2, steps)),
            dma((n, 2, steps)),
            dma((2 * XS,)),
            dma((2 * XS,)),
            dma((3,)),
            dma((3, n)),
            dma(()),
        ],
        compiler_params=pltpu.CompilerParams(
            collective_id=0, has_side_effects=True, vmem_limit_bytes=56 * 2**20
        ),
    )(prev_hidden, prev_cot, next_hidden, weight, moment1, moment2)


def solution(mesh):
    split = P(("node", "inner"), "tensor")
    return jax.shard_map(
        on_device,
        mesh=mesh,
        in_specs=(split, P(("node", "inner"), None), split, split, split, split),
        out_specs=(split,) * 4,
        check_vma=False,
    )
```

```python
import functools
import math

import jax
import jax.numpy as jnp
from jax import lax
from jax.experimental import pallas as pl
from jax.experimental.pallas import tpu as pltpu
from jax.sharding import PartitionSpec as P

FB = 14336
ADAM_STEP = 20
MESH = pl.DeviceIdType.MESH
XS = 4
CUT = 256
ORDER = ["C", "Y2", "X3", "Y3", "Y1", "X2", "G1", "G3", "R1", "A", "R3", "X1", "M", "O", "G2", "R2"]
DELAY = [3, 22, 6, 29, 16, 4, 21, 31, 8, 17, 11, 1, 6, 35, 25, 9]
SIDE = (0, 1, XS - 1, 2)


def kernel(
    zs, cut, order, delay,
    hid_ref, cot_ref, nxt_ref, w_ref, m1_ref, m2_ref,
    ffn_ref, nw_ref, nm1_ref, nm2_ref,
    hbuf, xbuf, cbuf, ct, grad, send_p, send_m, recv_p, recv_m, wv, m1v, m2v, wall, acc, part, got, fin,
    x_send, x_recv, x_own, c_send, c_recv, c_own, y_send, y_recv, rs_send, rs_recv, ag_send, ag_recv,
    o_send, o_recv, loads, stores, last,
):
    tok, cols = hid_ref.shape
    rows = w_ref.shape[0]
    n = cols // cut
    steps = zs // 2
    feats = rows * zs
    all_tokens = tok * zs * XS * 2
    factor = 1.0 / math.sqrt(FB)

    node, inner, ten = lax.axis_index("node"), lax.axis_index("inner"), lax.axis_index("tensor")
    core, x_lo, z = lax.rem(node, 2), lax.div(inner, zs), lax.rem(inner, zs)
    x = lax.div(node, 2) * 2 + x_lo

    def at(px, pz, pc, py):
        return (lax.div(px, 2) * 2 + pc, lax.rem(px, 2) * zs + pz, py)

    def row_peer(j, dc):
        return lax.rem(x + j, XS), lax.rem(core + dc, 2)

    def row_device(j, dc):
        px, pc = row_peer(j, dc)
        return at(px, z, pc, ten)

    def z_device(d):
        return at(x, lax.rem(z + d + zs, zs), core, ten)

    def y_device(d):
        return at(x, z, core, lax.rem(ten + d + 4, 4))

    barrier = pltpu.get_barrier_semaphore()
    at_home = node == ten
    for j in range(XS):
        for dc in range(2):
            if j or dc:
                pl.semaphore_signal(barrier, inc=1, device_id=row_device(j, dc), device_id_type=MESH)
    for d in (1, -1):
        pl.semaphore_signal(barrier, inc=1, device_id=z_device(d), device_id_type=MESH)
        pl.semaphore_signal(barrier, inc=1, device_id=y_device(d), device_id_type=MESH)
    for lo in range(2):
        for py in range(4):
            mine = at_home & (x_lo == lo) & (ten == py)

            @pl.when(jnp.logical_not(mine))
            def _():
                pl.semaphore_signal(
                    barrier, inc=1, device_id=(ten, lo * zs + z, jnp.int32(py)), device_id_type=MESH
                )

    load_w = pltpu.make_async_copy(w_ref, wv, loads.at[0])
    load_m1 = pltpu.make_async_copy(m1_ref, m1v, loads.at[1])
    load_m2 = pltpu.make_async_copy(m2_ref, m2v, loads.at[2])

    def block_of(px, pc):
        return (lax.div(px, 2) * 2 + pc) * 2 + lax.rem(px, 2)

    def cot_block(px, pc):
        return pl.ds(pl.multiple_of(block_of(px, pc) * feats, feats), feats)

    half, quarter = tok // 2, tok // 4
    parity = lax.rem(ten, 2)
    here_rows = pl.multiple_of(parity * half, half)
    there_rows = pl.multiple_of((1 - parity) * half, half)
    own_c = pltpu.make_async_copy(cot_ref.at[:, cot_block(x, core)], cbuf.at[0], c_own)

    def c_copy(i, dc):
        px, pc = row_peer(SIDE[i], dc)
        slot = 2 * (0, 2, 1, 3)[i] + dc
        part_rows = pl.ds(here_rows, half) if i else pl.ds(0, tok)
        return pltpu.make_async_remote_copy(
            src_ref=cot_ref.at[part_rows, cot_block(px, pc)], dst_ref=cbuf.at[slot, part_rows],
            send_sem=c_send.at[slot], recv_sem=c_recv.at[slot], device_id=at(px, z, pc, ten), device_id_type=MESH,
        )

    def y_copy(d, arriving=False):
        first = there_rows if arriving else here_rows
        ref = cbuf.at[2:2 * XS, pl.ds(pl.multiple_of(first + d * quarter, quarter), quarter)]
        return pltpu.make_async_remote_copy(
            src_ref=ref, dst_ref=ref, send_sem=y_send.at[d], recv_sem=y_recv.at[d],
            device_id=y_device(1 - 2 * d), device_id_type=MESH,
        )

    def chunk(k):
        return pl.ds(pl.multiple_of(k * cut, cut), cut)

    def x_own_copy(a, k):
        ref, buf = (hid_ref, hbuf) if a == 0 else (nxt_ref, xbuf)
        return pltpu.make_async_copy(ref.at[:, chunk(k)], buf.at[k, 0], x_own.at[a, k])

    def x_copy(a, k, i):
        ref, buf = (hid_ref, hbuf) if a == 0 else (nxt_ref, xbuf)
        first, second = pl.ds(0, half), pl.ds(half, half)
        src, dst, peer = {
            0: (ref.at[:, chunk(k)], buf.at[k, 1], (XS - 1, 0)),
            1: (ref.at[:, chunk(k)], buf.at[k, 2], (1, 0)),
            2: (buf.at[k, 2, first], buf.at[k, 3, first], (1, 0)),
            3: (buf.at[k, 1, second], buf.at[k, 3, second], (XS - 1, 0)),
            4: (buf.at[k, 0:XS], buf.at[k, XS:2 * XS], (0, 1)),
        }[i]
        return pltpu.make_async_remote_copy(
            src_ref=src, dst_ref=dst, send_sem=x_send.at[a, i], recv_sem=x_recv.at[a, k, i],
            device_id=row_device(*peer), device_id_type=MESH,
        )

    half_rows = rows // 2
    part_of = (pl.ds(0, half_rows), pl.ds(half_rows, half_rows))

    def rs_copy(k, d, s):
        src, dst = (send_p, recv_p) if d == 0 else (send_m, recv_m)
        src, dst = src.at[k, s], dst.at[k, s]
        if s == 0:
            src, dst = src.at[part_of[d]], dst.at[part_of[d]]
        return pltpu.make_async_remote_copy(
            src_ref=src, dst_ref=dst, send_sem=rs_send.at[d, s], recv_sem=rs_recv.at[k, d, s],
            device_id=z_device(1 - 2 * d), device_id_type=MESH,
        )

    def ag_copy(k, d, s, arriving=False):
        far = s + 1 if arriving else s
        slot = lax.rem(z + (zs - far if d == 0 else far), zs)
        ref = wall.at[k, slot]
        if s == steps - 1:
            ref = ref.at[part_of[d]]
        return pltpu.make_async_remote_copy(
            src_ref=ref, dst_ref=ref, send_sem=ag_send.at[d, s], recv_sem=ag_recv.at[k, d, s],
            device_id=z_device(1 - 2 * d), device_id_type=MESH,
        )

    def store(k, i):
        src, dst = ((wv, nw_ref), (m1v, nm1_ref), (m2v, nm2_ref))[i]
        return pltpu.make_async_copy(src.at[:, chunk(k)], dst.at[:, chunk(k)], stores.at[i])

    own_c.start()
    load_w.start()
    load_m1.start()
    load_m2.start()
    pl.semaphore_wait(barrier, 7 + 4 + 8 - jnp.where(at_home, 1, 0))
    for i in (3, 1, 2, 0):
        for dc in (0, 1):
            if i or dc:
                c_copy(i, dc).start()
    acc[...] = jnp.zeros_like(acc)

    def c_second(k):
        @pl.when(k == 0)
        def _():
            for i in (1, 2, 3):
                for dc in (0, 1):
                    c_copy(i, dc).wait_recv()
            y_copy(0).start()
            y_copy(1).start()

    def x_first(a, k):
        x_copy(a, k, 0).start()
        x_copy(a, k, 1).start()
        x_own_copy(a, k).start()

    def x_second(a, k):
        x_copy(a, k, 1).wait_recv()
        x_copy(a, k, 2).start()
        x_copy(a, k, 0).wait_recv()
        x_copy(a, k, 3).start()

    def x_third(a, k):
        x_own_copy(a, k).wait()
        x_copy(a, k, 2).wait_recv()
        x_copy(a, k, 3).wait_recv()
        x_copy(a, k, 4).start()

    def x_done(a, k):
        x_copy(a, k, 4).wait_recv()

    def multiply(k):
        @pl.when(k == 0)
        def _():
            own_c.wait()
            c_copy(0, 1).wait_recv()
            y_copy(0, arriving=True).wait_recv()
            y_copy(1, arriving=True).wait_recv()
            for i in range(XS):
                for dc in range(2):
                    place = (dc * XS + i) * tok
                    ct[:, place:place + tok] = cbuf[2 * i + dc].T

        x_done(0, k)
        block = hbuf[k].reshape(2 * XS * tok, cut)
        tile = min(4, zs)
        for i in range(zs // tile):
            sums = jnp.dot(
                ct[i * tile * rows:(i + 1) * tile * rows, :], block, preferred_element_type=jnp.float32
            )
            grad[k, i * tile:(i + 1) * tile] = sums.reshape(tile, rows, cut)
        opposite = grad[k, lax.rem(z + steps, zs)].astype(jnp.bfloat16)
        send_p[k, 0] = opposite
        send_m[k, 0] = opposite
        rs_copy(k, 0, 0).start()
        rs_copy(k, 1, 0).start()

    def rs_step(k, s):
        for d in range(2):
            src, dst = (send_p, recv_p) if d == 0 else (send_m, recv_m)
            rs_copy(k, d, s - 1).wait_recv()
            far = steps - s
            own = grad.at[k, lax.rem(z + (far if d == 0 else zs - far), zs)]
            if s == 1:
                with_it, without = (0, half_rows) if d == 0 else (half_rows, 0)
                a, b = pl.ds(with_it, half_rows), pl.ds(without, half_rows)
                src[k, s, a] = (own[a] + dst[k, 0, a].astype(jnp.float32)).astype(jnp.bfloat16)
                src[k, s, b] = own[b].astype(jnp.bfloat16)
            else:
                src[k, s] = (own[...] + dst[k, s - 1].astype(jnp.float32)).astype(jnp.bfloat16)
            rs_copy(k, d, s).start()

    def adam(k):
        @pl.when(k == 0)
        def _():
            load_w.wait()
            load_m1.wait()
            load_m2.wait()

        rs_copy(k, 0, steps - 1).wait_recv()
        rs_copy(k, 1, steps - 1).wait_recv()
        summed = (
            grad[k, z]
            + recv_p[k, steps - 1].astype(jnp.float32)
            + recv_m[k, steps - 1].astype(jnp.float32)
        )
        gradient = summed / all_tokens
        here = chunk(k)
        new_moment1 = 0.9 * m1v[:, here] + 0.1 * gradient
        new_moment2 = 0.95 * m2v[:, here] + 0.05 * gradient * gradient
        first_fix = 1.0 - 0.9**ADAM_STEP
        second_fix = 1.0 - 0.95**ADAM_STEP
        ratio = new_moment1 / first_fix / (jnp.sqrt(new_moment2 / second_fix) + 1e-08)
        weight = wv[:, here]
        new_weight = weight - 0.05 * (ratio + 0.1 * weight)
        wall[k, z] = new_weight.astype(jnp.bfloat16)
        ag_copy(k, 0, 0).start()
        ag_copy(k, 1, 0).start()
        wv[:, here] = new_weight
        m1v[:, here] = new_moment1
        m2v[:, here] = new_moment2
        for i in range(3):
            store(k, i).start()

    def ag_step(k, s):
        for d in range(2):
            ag_copy(k, d, s - 1, arriving=True).wait_recv()
            ag_copy(k, d, s).start()

    def forward(k):
        for d in range(2):
            ag_copy(k, d, steps - 1, arriving=True).wait_recv()
        x_done(1, k)

        pair = 2 - n % 2

        @pl.when(lax.rem(k, pair) == pair - 1)
        def _():
            copies = [wall[k - j].reshape(feats, cut) for j in range(pair)]
            for i in range(XS):
                mine = [xbuf[k - j, 2 * i:2 * i + 2].reshape(2 * tok, cut) for j in range(pair)]
                acc[2 * i * tok:2 * (i + 1) * tok, :] += sum(
                    lax.dot_general(a, b, (((1,), (1,)), ((), ())), preferred_element_type=jnp.float32)
                    for a, b in zip(mine, copies)
                )

    stages = {
        "C": c_second,
        "X1": functools.partial(x_first, 0),
        "X2": functools.partial(x_second, 0),
        "X3": functools.partial(x_third, 0),
        "Y1": functools.partial(x_first, 1),
        "Y2": functools.partial(x_second, 1),
        "Y3": functools.partial(x_third, 1),
        "M": multiply,
        "A": adam,
        "O": forward,
    }
    for s in range(1, steps):
        stages[f"R{s}"] = functools.partial(rs_step, s=s)
        stages[f"G{s}"] = functools.partial(ag_step, s=s)

    def tick(t, carry):
        for name, start in zip(order, delay):
            if name not in stages:
                continue
            k = t - start

            @pl.when((k >= 0) & (k < n))
            def _(k=k, stage=stages[name]):
                stage(k)

        return carry

    lax.fori_loop(0, max(delay) + n, tick, 0)

    def o_copy(i, dc):
        px, pc = row_peer(SIDE[i], dc)
        slot = XS * dc + i
        return pltpu.make_async_remote_copy(
            src_ref=part.at[slot], dst_ref=got.at[ten * 2 + x_lo], send_sem=o_send.at[slot],
            recv_sem=o_recv.at[ten * 2 + x_lo], device_id=at(px, z, pc, node), device_id_type=MESH,
        )

    stay = pltpu.make_async_copy(part.at[0], got.at[ten * 2 + x_lo], o_recv.at[ten * 2 + x_lo])
    for i in (3, 1, 2, 0):
        for dc in range(2):
            slot = XS * dc + i
            part[slot] = (acc[slot * tok:(slot + 1) * tok, :] * factor).astype(jnp.bfloat16)
            if slot:
                o_copy(i, dc).start()
            else:

                @pl.when(at_home)
                def _():
                    stay.start()

                @pl.when(jnp.logical_not(at_home))
                def _():
                    o_copy(0, 0).start()

    for i in range(XS):
        for dc in range(2):
            if i or dc:
                c_copy(i, dc).wait_send()
    for d in range(2):
        y_copy(d).wait_send()

    def all_sent(ref, sem):
        pltpu.make_async_copy(ref, ref, sem).wait()

    for a, buf in ((0, hbuf), (1, xbuf)):
        for i in range(2):
            all_sent(buf.at[:, 0], x_send.at[a, i])
        for i in range(2, 4):
            all_sent(buf.at[:, 0, pl.ds(0, half)], x_send.at[a, i])
        all_sent(buf.at[:, 0:XS], x_send.at[a, 4])
    for d in range(2):
        for s in range(steps):
            sent = send_p.at[:, s, part_of[0]] if s == 0 else send_p.at[:, s]
            all_sent(sent, rs_send.at[d, s])
            sent = send_p.at[:, 0, part_of[0]] if s == steps - 1 else send_p.at[:, 0]
            all_sent(sent, ag_send.at[d, s])
    for i, (src, dst) in enumerate(((wv, nw_ref), (m1v, nm1_ref), (m2v, nm2_ref))):
        pltpu.make_async_copy(src, dst, stores.at[i]).wait()

    for lo in range(2):
        total = jnp.zeros((tok, feats), jnp.float32)
        for py in range(4):
            slot = 2 * py + lo
            pltpu.make_async_copy(part.at[0], got.at[slot], o_recv.at[slot]).wait()
            total = total + got[slot].astype(jnp.float32)
        fin[:, lo * feats:(lo + 1) * feats] = total.astype(jnp.bfloat16)
    out = pltpu.make_async_copy(fin, ffn_ref, last)
    out.start()
    for i in range(XS):
        for dc in range(2):
            if i or dc:
                o_copy(i, dc).wait_send()

    @pl.when(jnp.logical_not(at_home))
    def _():
        o_copy(0, 0).wait_send()

    out.wait()


def hand_on(*refs):
    taken, given, held, (ins, outs) = refs[:4], refs[4:8], refs[8:12], refs[12:]
    moves = []
    for i in range(4):
        moves.append((
            pltpu.make_async_copy(taken[i], held[i], ins.at[i]),
            pltpu.make_async_copy(held[i], given[i], outs.at[i]),
        ))
    for read, _ in moves:
        read.start()
    for read, write in moves:
        read.wait()
        write.start()
    for _, write in moves:
        write.wait()


def on_device(prev_hidden, prev_cot, next_hidden, weight, moment1, moment2):
    tok, cols = prev_hidden.shape
    rows, features = weight.shape[0], prev_cot.shape[1]
    zs = lax.axis_size("inner") // 2
    steps = zs // 2
    cut = min(CUT, cols // 2)
    n = cols // cut
    feats = rows * zs
    bf16, f32 = jnp.bfloat16, jnp.float32
    dma = pltpu.SemaphoreType.DMA
    anywhere = pl.BlockSpec(memory_space=pl.ANY)
    outs = pl.pallas_call(
        functools.partial(kernel, zs, cut, ORDER, DELAY),
        out_shape=(
            jax.ShapeDtypeStruct((tok, features // 4), bf16),
            jax.ShapeDtypeStruct(weight.shape, f32),
            jax.ShapeDtypeStruct(weight.shape, f32),
            jax.ShapeDtypeStruct(weight.shape, f32),
        ),
        in_specs=[anywhere] * 6,
        out_specs=(anywhere,) * 4,
        scratch_shapes=[
            pltpu.VMEM((n, 2 * XS, tok, cut), bf16),
            pltpu.VMEM((n, 2 * XS, tok, cut), bf16),
            pltpu.VMEM((2 * XS, tok, feats), bf16),
            pltpu.VMEM((feats, 2 * XS * tok), bf16),
            pltpu.VMEM((n, zs, rows, cut), f32),
            pltpu.VMEM((n, steps, rows, cut), bf16),
            pltpu.VMEM((n, steps, rows, cut), bf16),
            pltpu.VMEM((n, steps, rows, cut), bf16),
            pltpu.VMEM((n, steps, rows, cut), bf16),
            pltpu.VMEM((rows, cols), f32),
            pltpu.VMEM((rows, cols), f32),
            pltpu.VMEM((rows, cols), f32),
            pltpu.VMEM((n, zs, rows, cut), bf16),
            pltpu.VMEM((2 * XS * tok, feats), f32),
            pltpu.VMEM((2 * XS, tok, feats), bf16),
            pltpu.VMEM((2 * XS, tok, feats), bf16),
            pltpu.VMEM((tok, 2 * feats), bf16),
            dma((2, 5)),
            dma((2, n, 5)),
            dma((2, n)),
            dma((2 * XS,)),
            dma((2 * XS,)),
            dma(()),
            dma((2,)),
            dma((2,)),
            dma((2, steps)),
            dma((n, 2, steps)),
            dma((2, steps)),
            dma((n, 2, steps)),
            dma((2 * XS,)),
            dma((2 * XS,)),
            dma((3,)),
            dma((3,)),
            dma(()),
        ],
        compiler_params=pltpu.CompilerParams(
            collective_id=0, has_side_effects=True, vmem_limit_bytes=56 * 2**20
        ),
    )(prev_hidden, prev_cot, next_hidden, weight, moment1, moment2)
    return pl.pallas_call(
        hand_on,
        out_shape=tuple(jax.ShapeDtypeStruct(o.shape, o.dtype) for o in outs),
        in_specs=[anywhere] * 4,
        out_specs=(anywhere,) * 4,
        scratch_shapes=[pltpu.VMEM(o.shape, o.dtype) for o in outs] + [dma((4,)), dma((4,))],
        compiler_params=pltpu.CompilerParams(vmem_limit_bytes=16 * 2**20),
    )(*outs)


def solution(mesh):
    split = P(("node", "inner"), "tensor")
    return jax.shard_map(
        on_device,
        mesh=mesh,
        in_specs=(split, P(("node", "inner"), None), split, split, split, split),
        out_specs=(split,) * 4,
        check_vma=False,
    )
```

```python
import functools
import math

import jax
import jax.numpy as jnp
from jax import lax
from jax.experimental import pallas as pl
from jax.experimental.pallas import tpu as pltpu
from jax.sharding import PartitionSpec as P

FB = 14336
ADAM_STEP = 20
MESH = pl.DeviceIdType.MESH
XS = 4
CUT = 256
ORDER = ["R2", "Y3", "Y1", "X1", "G3", "R1", "Y2", "M", "G2", "X3", "C", "A", "O", "G1", "R3", "X2"]
DELAY = [9, 30, 12, 0, 32, 7, 25, 5, 23, 4, 1, 13, 38, 18, 10, 2]
SIDE = (0, 1, XS - 1, 2)


def kernel(
    zs, cut, order, delay,
    hid_ref, cot_ref, nxt_ref, w_ref, m1_ref, m2_ref,
    ffn_ref, nw_ref, nm1_ref, nm2_ref,
    hbuf, xbuf, cbuf, ct, grad, send_p, send_m, recv_p, recv_m, wv, m1v, m2v, wall, acc, part, got, fin,
    x_send, x_recv, x_own, c_send, c_recv, c_own, y_send, y_recv, rs_send, rs_recv, ag_send, ag_recv,
    o_send, o_recv, loads, stores, last,
):
    tok, cols = hid_ref.shape
    rows = w_ref.shape[0]
    n = cols // cut
    steps = zs // 2
    feats = rows * zs
    all_tokens = tok * zs * XS * 2
    factor = 1.0 / math.sqrt(FB)

    node, inner, ten = lax.axis_index("node"), lax.axis_index("inner"), lax.axis_index("tensor")
    core, x_lo, z = lax.rem(node, 2), lax.div(inner, zs), lax.rem(inner, zs)
    x = lax.div(node, 2) * 2 + x_lo

    def at(px, pz, pc, py):
        return (lax.div(px, 2) * 2 + pc, lax.rem(px, 2) * zs + pz, py)

    def row_peer(j, dc):
        return lax.rem(x + j, XS), lax.rem(core + dc, 2)

    def row_device(j, dc):
        px, pc = row_peer(j, dc)
        return at(px, z, pc, ten)

    def z_device(d):
        return at(x, lax.rem(z + d + zs, zs), core, ten)

    def y_device(d):
        return at(x, z, core, lax.rem(ten + d + 4, 4))

    barrier = pltpu.get_barrier_semaphore()
    at_home = node == ten
    for j in range(XS):
        for dc in range(2):
            if j or dc:
                pl.semaphore_signal(barrier, inc=1, device_id=row_device(j, dc), device_id_type=MESH)
    for d in (1, -1):
        pl.semaphore_signal(barrier, inc=1, device_id=z_device(d), device_id_type=MESH)
        pl.semaphore_signal(barrier, inc=1, device_id=y_device(d), device_id_type=MESH)
    for lo in range(2):
        for py in range(4):
            mine = at_home & (x_lo == lo) & (ten == py)

            @pl.when(jnp.logical_not(mine))
            def _():
                pl.semaphore_signal(
                    barrier, inc=1, device_id=(ten, lo * zs + z, jnp.int32(py)), device_id_type=MESH
                )

    load_w = pltpu.make_async_copy(w_ref, wv, loads.at[0])
    load_m1 = pltpu.make_async_copy(m1_ref, m1v, loads.at[1])
    load_m2 = pltpu.make_async_copy(m2_ref, m2v, loads.at[2])

    def block_of(px, pc):
        return (lax.div(px, 2) * 2 + pc) * 2 + lax.rem(px, 2)

    def cot_block(px, pc):
        return pl.ds(pl.multiple_of(block_of(px, pc) * feats, feats), feats)

    half, quarter = tok // 2, tok // 4
    parity = lax.rem(ten, 2)
    here_rows = pl.multiple_of(parity * half, half)
    there_rows = pl.multiple_of((1 - parity) * half, half)
    own_c = pltpu.make_async_copy(cot_ref.at[:, cot_block(x, core)], cbuf.at[0], c_own)

    def c_copy(i, dc, p=0):
        px, pc = row_peer(SIDE[i], dc)
        slot = 2 * (0, 2, 1, 3)[i] + dc
        part_rows = pl.ds(pl.multiple_of(here_rows + p * quarter, quarter), quarter) if i else pl.ds(0, tok)
        return pltpu.make_async_remote_copy(
            src_ref=cot_ref.at[part_rows, cot_block(px, pc)], dst_ref=cbuf.at[slot, part_rows],
            send_sem=c_send.at[slot, p], recv_sem=c_recv.at[slot, p], device_id=at(px, z, pc, ten), device_id_type=MESH,
        )

    def y_copy(d, p, arriving=False):
        first = there_rows if arriving else here_rows
        eighth = quarter // 2
        ref = cbuf.at[2:2 * XS, pl.ds(pl.multiple_of(first + p * quarter + d * eighth, eighth), eighth)]
        return pltpu.make_async_remote_copy(
            src_ref=ref, dst_ref=ref, send_sem=y_send.at[d, p], recv_sem=y_recv.at[d, p],
            device_id=y_device(1 - 2 * d), device_id_type=MESH,
        )

    def chunk(k):
        return pl.ds(pl.multiple_of(k * cut, cut), cut)

    def x_own_copy(a, k):
        ref, buf = (hid_ref, hbuf) if a == 0 else (nxt_ref, xbuf)
        return pltpu.make_async_copy(ref.at[:, chunk(k)], buf.at[k, 0], x_own.at[a, k])

    def x_copy(a, k, i):
        ref, buf = (hid_ref, hbuf) if a == 0 else (nxt_ref, xbuf)
        first, second = pl.ds(0, half), pl.ds(half, half)
        src, dst, peer = {
            0: (ref.at[:, chunk(k)], buf.at[k, 1], (XS - 1, 0)),
            1: (ref.at[:, chunk(k)], buf.at[k, 2], (1, 0)),
            2: (buf.at[k, 2, first], buf.at[k, 3, first], (1, 0)),
            3: (buf.at[k, 1, second], buf.at[k, 3, second], (XS - 1, 0)),
            4: (buf.at[k, 0:XS], buf.at[k, XS:2 * XS], (0, 1)),
        }[i]
        return pltpu.make_async_remote_copy(
            src_ref=src, dst_ref=dst, send_sem=x_send.at[a, i], recv_sem=x_recv.at[a, k, i],
            device_id=row_device(*peer), device_id_type=MESH,
        )

    half_rows = rows // 2
    part_of = (pl.ds(0, half_rows), pl.ds(half_rows, half_rows))

    def rs_copy(k, d, s):
        src, dst = (send_p, recv_p) if d == 0 else (send_m, recv_m)
        src, dst = src.at[k, s], dst.at[k, s]
        if s == 0:
            src, dst = src.at[part_of[d]], dst.at[part_of[d]]
        return pltpu.make_async_remote_copy(
            src_ref=src, dst_ref=dst, send_sem=rs_send.at[d, s], recv_sem=rs_recv.at[k, d, s],
            device_id=z_device(1 - 2 * d), device_id_type=MESH,
        )

    def ag_copy(k, d, s, arriving=False):
        far = s + 1 if arriving else s
        slot = lax.rem(z + (zs - far if d == 0 else far), zs)
        ref = wall.at[k, slot]
        if s == steps - 1:
            ref = ref.at[part_of[d]]
        return pltpu.make_async_remote_copy(
            src_ref=ref, dst_ref=ref, send_sem=ag_send.at[d, s], recv_sem=ag_recv.at[k, d, s],
            device_id=z_device(1 - 2 * d), device_id_type=MESH,
        )

    def store(k, i):
        src, dst = ((wv, nw_ref), (m1v, nm1_ref), (m2v, nm2_ref))[i]
        return pltpu.make_async_copy(src.at[:, chunk(k)], dst.at[:, chunk(k)], stores.at[i])

    own_c.start()
    load_w.start()
    load_m1.start()
    load_m2.start()
    pl.semaphore_wait(barrier, 7 + 4 + 8 - jnp.where(at_home, 1, 0))
    for p in range(2):
        for i in (3, 1, 2):
            for dc in (0, 1):
                c_copy(i, dc, p).start()
    c_copy(0, 1).start()
    acc[...] = jnp.zeros_like(acc)

    def c_second(k):
        for p in range(2):

            @pl.when(k == p)
            def _(p=p):
                for i in (1, 2, 3):
                    for dc in (0, 1):
                        c_copy(i, dc, p).wait_recv()
                y_copy(0, p).start()
                y_copy(1, p).start()

    def x_first(a, k):
        x_copy(a, k, 0).start()
        x_copy(a, k, 1).start()
        x_own_copy(a, k).start()

    def x_second(a, k):
        x_copy(a, k, 1).wait_recv()
        x_copy(a, k, 2).start()
        x_copy(a, k, 0).wait_recv()
        x_copy(a, k, 3).start()

    def x_third(a, k):
        x_own_copy(a, k).wait()
        x_copy(a, k, 2).wait_recv()
        x_copy(a, k, 3).wait_recv()
        x_copy(a, k, 4).start()

    def x_done(a, k):
        x_copy(a, k, 4).wait_recv()

    def multiply(k):
        @pl.when(k == 0)
        def _():
            own_c.wait()
            c_copy(0, 1).wait_recv()
            for i in range(XS):
                if i == 1:
                    for p in range(2):
                        for d in range(2):
                            y_copy(d, p, arriving=True).wait_recv()
                for dc in range(2):
                    place = (dc * XS + i) * tok
                    ct[:, place:place + tok] = cbuf[2 * i + dc].T

        x_done(0, k)
        block = hbuf[k].reshape(2 * XS * tok, cut)
        tile = min(4, zs)
        for i in range(zs // tile):
            sums = jnp.dot(
                ct[i * tile * rows:(i + 1) * tile * rows, :], block, preferred_element_type=jnp.float32
            )
            grad[k, i * tile:(i + 1) * tile] = sums.reshape(tile, rows, cut)
        opposite = grad[k, lax.rem(z + steps, zs)].astype(jnp.bfloat16)
        send_p[k, 0] = opposite
        send_m[k, 0] = opposite
        rs_copy(k, 0, 0).start()
        rs_copy(k, 1, 0).start()

    def rs_step(k, s):
        for d in range(2):
            src, dst = (send_p, recv_p) if d == 0 else (send_m, recv_m)
            rs_copy(k, d, s - 1).wait_recv()
            far = steps - s
            own = grad.at[k, lax.rem(z + (far if d == 0 else zs - far), zs)]
            if s == 1:
                with_it, without = (0, half_rows) if d == 0 else (half_rows, 0)
                a, b = pl.ds(with_it, half_rows), pl.ds(without, half_rows)
                src[k, s, a] = (own[a] + dst[k, 0, a].astype(jnp.float32)).astype(jnp.bfloat16)
                src[k, s, b] = own[b].astype(jnp.bfloat16)
            else:
                src[k, s] = (own[...] + dst[k, s - 1].astype(jnp.float32)).astype(jnp.bfloat16)
            rs_copy(k, d, s).start()

    def adam(k):
        @pl.when(k == 0)
        def _():
            load_w.wait()
            load_m1.wait()
            load_m2.wait()

        rs_copy(k, 0, steps - 1).wait_recv()
        rs_copy(k, 1, steps - 1).wait_recv()
        summed = (
            grad[k, z]
            + recv_p[k, steps - 1].astype(jnp.float32)
            + recv_m[k, steps - 1].astype(jnp.float32)
        )
        gradient = summed / all_tokens
        here = chunk(k)
        new_moment1 = 0.9 * m1v[:, here] + 0.1 * gradient
        new_moment2 = 0.95 * m2v[:, here] + 0.05 * gradient * gradient
        first_fix = 1.0 - 0.9**ADAM_STEP
        second_fix = 1.0 - 0.95**ADAM_STEP
        ratio = new_moment1 / first_fix / (jnp.sqrt(new_moment2 / second_fix) + 1e-08)
        weight = wv[:, here]
        new_weight = weight - 0.05 * (ratio + 0.1 * weight)
        wall[k, z] = new_weight.astype(jnp.bfloat16)
        ag_copy(k, 0, 0).start()
        ag_copy(k, 1, 0).start()
        wv[:, here] = new_weight
        m1v[:, here] = new_moment1
        m2v[:, here] = new_moment2
        for i in range(3):
            store(k, i).start()

    def ag_step(k, s):
        for d in range(2):
            ag_copy(k, d, s - 1, arriving=True).wait_recv()
            ag_copy(k, d, s).start()

    def forward(k):
        for d in range(2):
            ag_copy(k, d, steps - 1, arriving=True).wait_recv()
        x_done(1, k)

        pair = 2 - n % 2

        @pl.when(lax.rem(k, pair) == pair - 1)
        def _():
            copies = [wall[k - j].reshape(feats, cut) for j in range(pair)]
            for i in range(XS):
                mine = [xbuf[k - j, 2 * i:2 * i + 2].reshape(2 * tok, cut) for j in range(pair)]
                acc[2 * i * tok:2 * (i + 1) * tok, :] += sum(
                    lax.dot_general(a, b, (((1,), (1,)), ((), ())), preferred_element_type=jnp.float32)
                    for a, b in zip(mine, copies)
                )

    stages = {
        "C": c_second,
        "X1": functools.partial(x_first, 0),
        "X2": functools.partial(x_second, 0),
        "X3": functools.partial(x_third, 0),
        "Y1": functools.partial(x_first, 1),
        "Y2": functools.partial(x_second, 1),
        "Y3": functools.partial(x_third, 1),
        "M": multiply,
        "A": adam,
        "O": forward,
    }
    for s in range(1, steps):
        stages[f"R{s}"] = functools.partial(rs_step, s=s)
        stages[f"G{s}"] = functools.partial(ag_step, s=s)

    def tick(t, carry):
        for name, start in zip(order, delay):
            if name not in stages:
                continue
            k = t - start

            @pl.when((k >= 0) & (k < n))
            def _(k=k, stage=stages[name]):
                stage(k)

        return carry

    lax.fori_loop(0, max(delay) + n, tick, 0)

    def o_copy(i, dc):
        px, pc = row_peer(SIDE[i], dc)
        slot = XS * dc + i
        return pltpu.make_async_remote_copy(
            src_ref=part.at[slot], dst_ref=got.at[ten * 2 + x_lo], send_sem=o_send.at[slot],
            recv_sem=o_recv.at[ten * 2 + x_lo], device_id=at(px, z, pc, node), device_id_type=MESH,
        )

    stay = pltpu.make_async_copy(part.at[0], got.at[ten * 2 + x_lo], o_recv.at[ten * 2 + x_lo])
    for i in (3, 1, 2, 0):
        for dc in range(2):
            slot = XS * dc + i
            part[slot] = (acc[slot * tok:(slot + 1) * tok, :] * factor).astype(jnp.bfloat16)
            if slot:
                o_copy(i, dc).start()
            else:

                @pl.when(at_home)
                def _():
                    stay.start()

                @pl.when(jnp.logical_not(at_home))
                def _():
                    o_copy(0, 0).start()

    c_copy(0, 1).wait_send()
    for p in range(2):
        for i in range(1, XS):
            for dc in range(2):
                c_copy(i, dc, p).wait_send()
        for d in range(2):
            y_copy(d, p).wait_send()

    def all_sent(ref, sem):
        pltpu.make_async_copy(ref, ref, sem).wait()

    for a, buf in ((0, hbuf), (1, xbuf)):
        for i in range(2):
            all_sent(buf.at[:, 0], x_send.at[a, i])
        for i in range(2, 4):
            all_sent(buf.at[:, 0, pl.ds(0, half)], x_send.at[a, i])
        all_sent(buf.at[:, 0:XS], x_send.at[a, 4])
    for d in range(2):
        for s in range(steps):
            sent = send_p.at[:, s, part_of[0]] if s == 0 else send_p.at[:, s]
            all_sent(sent, rs_send.at[d, s])
            sent = send_p.at[:, 0, part_of[0]] if s == steps - 1 else send_p.at[:, 0]
            all_sent(sent, ag_send.at[d, s])
    for i, (src, dst) in enumerate(((wv, nw_ref), (m1v, nm1_ref), (m2v, nm2_ref))):
        pltpu.make_async_copy(src, dst, stores.at[i]).wait()

    def done(lo):
        here = pl.ds(lo * feats, feats)
        return pltpu.make_async_copy(fin.at[:, here], ffn_ref.at[:, here], last.at[lo])

    for lo in range(2):
        total = jnp.zeros((tok, feats), jnp.float32)
        for py in range(4):
            slot = 2 * py + lo
            pltpu.make_async_copy(part.at[0], got.at[slot], o_recv.at[slot]).wait()
            total = total + got[slot].astype(jnp.float32)
        fin[:, lo * feats:(lo + 1) * feats] = total.astype(jnp.bfloat16)
        done(lo).start()
    for i in range(XS):
        for dc in range(2):
            if i or dc:
                o_copy(i, dc).wait_send()

    @pl.when(jnp.logical_not(at_home))
    def _():
        o_copy(0, 0).wait_send()

    for lo in range(2):
        done(lo).wait()


def hand_on(*refs):
    taken, given, held, (ins, outs) = refs[:4], refs[4:8], refs[8:12], refs[12:]
    moves = []
    for i in range(4):
        moves.append((
            pltpu.make_async_copy(taken[i], held[i], ins.at[i]),
            pltpu.make_async_copy(held[i], given[i], outs.at[i]),
        ))
    for read, _ in moves:
        read.start()
    for read, write in moves:
        read.wait()
        write.start()
    for _, write in moves:
        write.wait()


def on_device(prev_hidden, prev_cot, next_hidden, weight, moment1, moment2):
    tok, cols = prev_hidden.shape
    rows, features = weight.shape[0], prev_cot.shape[1]
    zs = lax.axis_size("inner") // 2
    steps = zs // 2
    cut = min(CUT, cols // 2)
    n = cols // cut
    feats = rows * zs
    bf16, f32 = jnp.bfloat16, jnp.float32
    dma = pltpu.SemaphoreType.DMA
    anywhere = pl.BlockSpec(memory_space=pl.ANY)
    outs = pl.pallas_call(
        functools.partial(kernel, zs, cut, ORDER, DELAY),
        out_shape=(
            jax.ShapeDtypeStruct((tok, features // 4), bf16),
            jax.ShapeDtypeStruct(weight.shape, f32),
            jax.ShapeDtypeStruct(weight.shape, f32),
            jax.ShapeDtypeStruct(weight.shape, f32),
        ),
        in_specs=[anywhere] * 6,
        out_specs=(anywhere,) * 4,
        scratch_shapes=[
            pltpu.VMEM((n, 2 * XS, tok, cut), bf16),
            pltpu.VMEM((n, 2 * XS, tok, cut), bf16),
            pltpu.VMEM((2 * XS, tok, feats), bf16),
            pltpu.VMEM((feats, 2 * XS * tok), bf16),
            pltpu.VMEM((n, zs, rows, cut), f32),
            pltpu.VMEM((n, steps, rows, cut), bf16),
            pltpu.VMEM((n, steps, rows, cut), bf16),
            pltpu.VMEM((n, steps, rows, cut), bf16),
            pltpu.VMEM((n, steps, rows, cut), bf16),
            pltpu.VMEM((rows, cols), f32),
            pltpu.VMEM((rows, cols), f32),
            pltpu.VMEM((rows, cols), f32),
            pltpu.VMEM((n, zs, rows, cut), bf16),
            pltpu.VMEM((2 * XS * tok, feats), f32),
            pltpu.VMEM((2 * XS, tok, feats), bf16),
            pltpu.VMEM((2 * XS, tok, feats), bf16),
            pltpu.VMEM((tok, 2 * feats), bf16),
            dma((2, 5)),
            dma((2, n, 5)),
            dma((2, n)),
            dma((2 * XS, 2)),
            dma((2 * XS, 2)),
            dma(()),
            dma((2, 2)),
            dma((2, 2)),
            dma((2, steps)),
            dma((n, 2, steps)),
            dma((2, steps)),
            dma((n, 2, steps)),
            dma((2 * XS,)),
            dma((2 * XS,)),
            dma((3,)),
            dma((3,)),
            dma((2,)),
        ],
        compiler_params=pltpu.CompilerParams(
            collective_id=0, has_side_effects=True, vmem_limit_bytes=56 * 2**20
        ),
    )(prev_hidden, prev_cot, next_hidden, weight, moment1, moment2)
    return pl.pallas_call(
        hand_on,
        out_shape=tuple(jax.ShapeDtypeStruct(o.shape, o.dtype) for o in outs),
        in_specs=[anywhere] * 4,
        out_specs=(anywhere,) * 4,
        scratch_shapes=[pltpu.VMEM(o.shape, o.dtype) for o in outs] + [dma((4,)), dma((4,))],
        compiler_params=pltpu.CompilerParams(vmem_limit_bytes=16 * 2**20),
    )(*outs)


def solution(mesh):
    split = P(("node", "inner"), "tensor")
    return jax.shard_map(
        on_device,
        mesh=mesh,
        in_specs=(split, P(("node", "inner"), None), split, split, split, split),
        out_specs=(split,) * 4,
        check_vma=False,
    )
```
